32 devices in a mesh: parts: 2 (over y), node: 4 (over z), local: 4 (over x, core).
Axes of the slice: x: 2, y: 2, z: 4, core: 2. Of those that a mesh axis runs over, the one named last changes fastest.
Arguments:
- tokens: bfloat16 [2048, 3584], P(('parts', 'node', 'local')), parts along dimension 0, may hold values from -6 to 6
- expert_ids: int32 [2048, 8], P(('parts', 'node', 'local')), parts along dimension 0, may hold values from 0 to 7, as said below
- gate_scores: bfloat16 [2048, 8], P(('parts', 'node', 'local')), parts along dimension 0, may hold values from 0.19921875 to 1
- gate_weight: bfloat16 [16, 3584, 512], P(('node', 'local')), may hold values from -0.09375 to 0.09375
- up_weight: bfloat16 [16, 3584, 512], P(('node', 'local')), may hold values from -0.09375 to 0.09375
- down_weight: bfloat16 [16, 512, 3584], P(('node', 'local')), may hold values from -0.1875 to 0.1875
Outputs:
- combined: bfloat16 [2048, 3584], P(('parts', 'node', 'local')), parts along dimension 0
The draws below stay inside these ranges and needn't reach their ends.
There are 2 independent parts, one for each index of `parts`. The reference program is written for one: setup_inputs(seed, part) draws one part's arguments, and reference() takes and returns one part's arrays. A program takes and returns all parts, laid end to end along the dimension named above; an argument that names none is the same for every part. Nothing has to cross between parts.
Inputs may be any that keep to these rules, and one draw needn't show every extreme that they name: `expert_ids`: each token names 8 different experts, two from each of exactly 4 groups, in any order. Among the 64 tokens of one device each group is named by exactly 64 tokens and no expert by more than 64. In every group one expert, the same on every device of a part, is named by exactly 64 tokens of every device.
All inputs are finite; a program needn't handle non-finite values.
Results may differ from the reference program's by a relative error of at most 0.0072.
Values may be sent and summed in bfloat16 or wider, within the bound.
No kernel may reach another device: no remote copies, remote signals or barrier semaphores. Data moves between devices by JAX's collectives and lax.ppermute only.
A program may use at most 128 MiB of HBM per device.

```python
import math
import jax
import jax.numpy as jnp
from jax import lax

D = 3584
FF = 1024
HALF = 512
TOPK = 8
TOPG = 4
TOK_DEV = 64
TOKENS = 1024
EXP_GROUP = 2
EXPERTS = 8
CHOOSERS = 64
MOST = 64
N_NODE = 4
N_LOCAL = 4


def route_block(block_key, hot_slots):
    first_key, second_key, third_key, fourth_key, fifth_key = jax.random.split(block_key, 5)
    order = jax.random.permutation(first_key, TOK_DEV)
    group_order = jax.random.permutation(second_key, N_NODE)
    residue = order % N_NODE
    within = order // N_NODE
    per_residue = TOK_DEV // N_NODE
    offsets = jnp.arange(TOPG)
    chosen_group = group_order[(residue[:, None] + offsets[None, :]) % N_NODE]
    standing = offsets[None, :] * per_residue + within[:, None]
    cold = EXP_GROUP - 1
    rest = 2 * CHOOSERS - MOST
    base = rest // cold
    extra = rest % cold
    drawn = base + (jnp.arange(cold) < extra).astype(jnp.int32)
    limit = max(0, min(base, MOST - base - 1))
    pair_count = cold // 2
    moves = jax.random.randint(third_key, (N_NODE, pair_count), 0, limit + 1)
    paired = jnp.stack([moves, -moves], axis=-1).reshape(N_NODE, 2 * pair_count)
    delta = jnp.pad(paired, ((0, 0), (0, cold - 2 * pair_count)))
    counts_cold = drawn[None, :] + delta
    counts = jnp.concatenate([jnp.full((N_NODE, 1), MOST, jnp.int32), counts_cold.astype(jnp.int32)], axis=1)
    ends = jnp.cumsum(counts, axis=1)
    places = jnp.arange(2 * CHOOSERS)
    rank_at = jnp.sum((ends[:, None, :] <= places[None, :, None]).astype(jnp.int32), axis=-1)
    cold_perm = jax.vmap(lambda piece_key: jax.random.permutation(piece_key, cold))(jax.random.split(fourth_key, N_NODE))
    slot_of_rank = jnp.concatenate([hot_slots[:, None], (hot_slots[:, None] + 1 + cold_perm) % EXP_GROUP], axis=1)
    first_rank = rank_at[chosen_group, standing]
    second_rank = rank_at[chosen_group, standing + CHOOSERS]
    first_slot = slot_of_rank[chosen_group, first_rank]
    second_slot = slot_of_rank[chosen_group, second_rank]
    picks = jnp.stack([chosen_group * EXP_GROUP + first_slot, chosen_group * EXP_GROUP + second_slot], axis=-1).reshape(TOK_DEV, TOPK)
    column_orders = jax.vmap(lambda piece_key: jax.random.permutation(piece_key, TOPK))(jax.random.split(fifth_key, TOK_DEV))
    return jnp.take_along_axis(picks, column_orders, axis=1)


def draw_expert_ids(key, part):
    key = jax.random.fold_in(key, 7)
    hot_key, block_key = jax.random.split(key, 2)
    hot_slots = jax.random.randint(hot_key, (N_NODE,), 0, EXP_GROUP)
    block_keys = jax.random.split(block_key, N_NODE * N_LOCAL)
    blocks = jax.vmap(lambda piece_key: route_block(piece_key, hot_slots))(block_keys)
    return blocks.reshape(TOKENS, TOPK).astype(jnp.int32)


def steps_of(rng, dims, cuts, low, top_value):
    gain, own = 1.0, jax.random.fold_in(rng, 6)
    for dim, parts in cuts:
        steps = jnp.exp(jax.random.uniform(jax.random.fold_in(own, dim), (parts,), jnp.float32, low / len(cuts), top_value / len(cuts)))
        gain = gain * jnp.repeat(steps, dims[dim] // parts).reshape([-1 if axis == dim else 1 for axis in range(len(dims))])
    return gain


def normal_values(own_key, extent, width, most, cuts=(), dtype=jnp.bfloat16):
    result = width * jax.random.normal(own_key, extent, jnp.float32)
    if cuts:
        result = result * steps_of(own_key, extent, cuts, -0.22, 0.18)
    return jnp.clip(result, -most, most).astype(dtype)


def setup_inputs(seed: int = 0, part: int = 0) -> dict:
    keys = jax.random.split(jax.random.key(seed), 7)
    part_keys = jax.random.split(jax.random.fold_in(keys[6], part), 7)
    tokens = normal_values(part_keys[0], (TOKENS, D), 1.0, 6.0, ((0, 16),))
    expert_ids = draw_expert_ids(jax.random.fold_in(jax.random.fold_in(keys[6], part), 71), part)
    gate_scores = jnp.clip(jnp.exp(math.log(1.0) - 1.6133518 * jax.random.uniform(part_keys[2], (TOKENS, TOPK), jnp.float32) ** steps_of(part_keys[2], (TOKENS, TOPK), ((0, 16),), -0.2, 0.2)), 0.19921875, 1.0).astype(jnp.bfloat16)
    gate_weight = normal_values(keys[3], (2 * EXPERTS, D, HALF), D ** -0.5, 0.09375, ((0, 16),))
    up_weight = normal_values(keys[4], (2 * EXPERTS, D, HALF), D ** -0.5, 0.09375, ((0, 16),))
    down_weight = normal_values(keys[5], (2 * EXPERTS, HALF, D), FF ** -0.5, 0.1875, ((0, 16),))
    return {"tokens": tokens, "expert_ids": expert_ids, "gate_scores": gate_scores, "gate_weight": gate_weight, "up_weight": up_weight, "down_weight": down_weight}


def expert_half(picked, position, gate_weight, up_weight, down_weight):
    gate_mat = lax.dynamic_index_in_dim(gate_weight, position, 0, keepdims=False)
    up_mat = lax.dynamic_index_in_dim(up_weight, position, 0, keepdims=False)
    down_mat = lax.dynamic_index_in_dim(down_weight, position, 0, keepdims=False)
    gate_act = jnp.dot(picked, gate_mat, preferred_element_type=jnp.float32)
    up_act = jnp.dot(picked, up_mat, preferred_element_type=jnp.float32)
    hidden = (jax.nn.silu(gate_act) * up_act).astype(jnp.bfloat16)
    return jnp.dot(hidden, down_mat, preferred_element_type=jnp.float32).astype(jnp.bfloat16)


def reference(tokens, expert_ids, gate_scores, gate_weight, up_weight, down_weight):
    capacity = N_NODE * N_LOCAL * MOST
    places = jnp.arange(capacity)
    scores_wide = gate_scores.astype(jnp.float32)
    combined = jnp.zeros(tokens.shape, jnp.float32)
    for group_index in range(N_NODE):
        def add_expert(member, running):
            expert = group_index * EXP_GROUP + member
            naming = expert_ids == expert
            weight = jnp.sum(jnp.where(naming, scores_wide, jnp.float32(0.0)), axis=1)
            chosen = jnp.any(naming, axis=1)
            position = jnp.nonzero(chosen, size=capacity, fill_value=0)[0].astype(jnp.int32)
            filled = places < jnp.sum(chosen.astype(jnp.int32))
            picked = tokens[position]
            lower_half = expert_half(picked, 2 * expert, gate_weight, up_weight, down_weight)
            second = expert_half(picked, 2 * expert + 1, gate_weight, up_weight, down_weight)
            summed = (lower_half.astype(jnp.float32) + second.astype(jnp.float32)).astype(jnp.bfloat16)
            output = lax.optimization_barrier(summed).astype(jnp.float32)
            factor = jnp.where(filled, weight[position], jnp.float32(0.0))
            return running.at[position].add(output * factor[:, None])

        running = lax.fori_loop(0, EXP_GROUP, add_expert, jnp.zeros(tokens.shape, jnp.float32))
        rounded = lax.optimization_barrier(running.astype(jnp.bfloat16))
        combined = combined + rounded.astype(jnp.float32)
    return combined.astype(jnp.bfloat16)
```

```python
import functools

import jax
import jax.numpy as jnp
from jax import lax
from jax.experimental import pallas as pl
from jax.experimental.pallas import tpu as pltpu
from jax.sharding import PartitionSpec as P

TOPG = 4


def partner(value, axis, bit):
    mask = 2**bit
    pairs = [(source, source ^ mask) for source in range(lax.axis_size(axis))]
    return lax.ppermute(value, axis, pairs)


def expert_apply(arrived, gate_weight, up_weight, down_weight):
    layout = arrived.shape
    flat_rows = arrived.reshape(-1, layout[-1])
    gate_act = jnp.dot(flat_rows, gate_weight[0], preferred_element_type=jnp.float32)
    up_act = jnp.dot(flat_rows, up_weight[0], preferred_element_type=jnp.float32)
    hidden = (jax.nn.silu(gate_act) * up_act).astype(jnp.bfloat16)
    result = jnp.dot(hidden, down_weight[0], preferred_element_type=jnp.float32).astype(
        jnp.bfloat16
    )
    return result.reshape(layout)


def routed(tokens, expert_ids, gate_scores, gate_weight, up_weight, down_weight):
    rows_dev, model_width = tokens.shape
    node_count = lax.axis_size("node")
    local_count = lax.axis_size("local")
    per_group = local_count // 2
    chooser_cap = rows_dev * TOPG // node_count
    bound_most = min(chooser_cap, 3 * chooser_cap // per_group)
    group_ids = jnp.arange(node_count)
    owner_group = expert_ids // per_group
    chosen = jnp.any(owner_group[:, :, None] == group_ids[None, None, :], axis=1)
    chosen_int = chosen.astype(jnp.int32)
    before = jnp.cumsum(chosen_int, axis=0) - chosen_int
    select_one = chosen.T[:, None, :] & (
        before.T[:, None, :] == jnp.arange(chooser_cap)[None, :, None]
    )
    one_hot = select_one.astype(jnp.bfloat16)
    send_rows = jnp.einsum(
        "gsb,bd->gsd", one_hot, tokens, preferred_element_type=jnp.float32
    ).astype(jnp.bfloat16)
    token_at = jnp.sum(jnp.where(select_one, jnp.arange(rows_dev)[None, None, :], 0), axis=-1)
    occupied = jnp.any(select_one, axis=-1)
    inside = (owner_group[token_at] == group_ids[:, None, None]) & occupied[:, :, None]
    send_ids = jnp.where(inside, expert_ids[token_at] % per_group, -1)
    send_scores = jnp.where(inside, gate_scores[token_at], 0)
    arrived_rows, arrived_ids, arrived_scores = (
        lax.all_to_all(send_rows, "node", split_axis=0, concat_axis=0, tiled=True),
        lax.all_to_all(send_ids, "node", split_axis=0, concat_axis=0, tiled=True),
        lax.all_to_all(send_scores, "node", split_axis=0, concat_axis=0, tiled=True),
    )
    relayed = node_count * chooser_cap
    relay_rows = arrived_rows.reshape(relayed, model_width)
    relay_ids = arrived_ids.reshape(relayed, -1)
    relay_scores = arrived_scores.reshape(relayed, -1).astype(jnp.float32)
    member_ids = jnp.arange(per_group)
    matches = relay_ids[:, :, None] == member_ids[None, None, :]
    naming = jnp.any(matches, axis=1)
    naming_int = naming.astype(jnp.int32)
    ahead_count = jnp.cumsum(naming_int, axis=0) - naming_int
    group_cap = node_count * bound_most
    half_cap = group_cap // 2
    select_two = naming.T[:, None, :] & (
        ahead_count.T[:, None, :] == jnp.arange(group_cap)[None, :, None]
    )
    expert_rows = jnp.einsum(
        "jsr,rd->jsd",
        select_two.astype(jnp.bfloat16),
        relay_rows,
        preferred_element_type=jnp.float32,
    ).astype(jnp.bfloat16)
    outbound = expert_rows.reshape(local_count, half_cap, model_width)
    arrived = lax.all_to_all(outbound, "local", split_axis=0, concat_axis=0, tiled=True)
    partner_rows = partner(arrived, "local", 0)
    stacked = jnp.concatenate([arrived, partner_rows], axis=0)
    outputs = expert_apply(stacked, gate_weight, up_weight, down_weight)
    count = arrived.shape[0]
    mine = outputs[:count]
    theirs = outputs[count:]
    back = partner(theirs, "local", 0)
    partials = (mine.astype(jnp.float32) + back.astype(jnp.float32)).astype(jnp.bfloat16)
    returned = lax.all_to_all(partials, "local", split_axis=0, concat_axis=0, tiled=True)
    relay_weight = jnp.sum(jnp.where(matches, relay_scores[:, :, None], 0.0), axis=1)
    weighted = (jnp.transpose(select_two, (2, 0, 1)) * relay_weight[:, :, None]).astype(
        jnp.bfloat16
    )
    expert_output = returned.reshape(per_group, group_cap, model_width)
    group_sum = jnp.einsum(
        "rjs,jsd->rd", weighted, expert_output, preferred_element_type=jnp.float32
    ).astype(jnp.bfloat16)
    gathered_back = lax.all_to_all(
        group_sum.reshape(node_count, chooser_cap, model_width),
        "node",
        split_axis=0,
        concat_axis=0,
        tiled=True,
    )
    combined = jnp.einsum("gsb,gsd->bd", one_hot, gathered_back, preferred_element_type=jnp.float32)
    return combined.astype(jnp.bfloat16)

def expert_kernel(count, down_tiles, hidden_tile, *refs):
    blocks, scores, weights = refs[:count], refs[count], refs[count + 1 : count + 7]
    outs = refs[count + 7 : 2 * count + 7]
    rows_all, gate, up, down, hidden, sems = refs[2 * count + 7 :]
    rows, width = blocks[0].shape
    half = gate.shape[-1]
    started = []

    def fetch(source, target):
        copy = pltpu.make_async_copy(source, target, sems.at[len(started)])
        copy.start()
        started.append(copy)
        return copy

    first, second = [], []
    for side in range(2):
        gate_hbm, up_hbm, _ = weights[3 * side : 3 * side + 3]
        for start in range(0, half, hidden_tile):
            cols = pl.ds(start, hidden_tile)
            pair = (
                fetch(gate_hbm.at[0, :, cols], gate.at[side, :, cols]),
                fetch(up_hbm.at[0, :, cols], up.at[side, :, cols]),
            )
            first.append((side, cols, pair))
    step = width // down_tiles
    for start in range(0, width, step):
        cols = pl.ds(start, step)
        pair = tuple(
            fetch(weights[3 * side + 2].at[0, :, cols], down.at[side, :, cols]) for side in range(2)
        )
        second.append((cols, pair))
    for i in range(count):
        rows_all[pl.ds(i * rows, rows), :] = blocks[i][...]
    for side, cols, pair in first:
        for copy in pair:
            copy.wait()
        gate_act = jnp.dot(rows_all[...], gate[side, :, cols], preferred_element_type=jnp.float32)
        up_act = jnp.dot(rows_all[...], up[side, :, cols], preferred_element_type=jnp.float32)
        hidden[side, :, cols] = (jax.nn.silu(gate_act) * up_act).astype(jnp.bfloat16)
    for cols, pair in second:
        for copy in pair:
            copy.wait()
        result = jnp.dot(hidden[0], down[0, :, cols], preferred_element_type=jnp.float32)
        result += jnp.dot(hidden[1], down[1, :, cols], preferred_element_type=jnp.float32)
        result = (result * scores[...]).astype(jnp.bfloat16)
        for i in range(count):
            outs[i][:, cols] = result[i * rows : (i + 1) * rows]


def expert_rows(blocks, scores, own, other):
    count = len(blocks)
    rows, width = blocks[0].shape
    half = own[0].shape[-1]
    total = count * rows
    down_tiles = 4
    hidden_tile = half // 2
    vmem = pl.BlockSpec(memory_space=pltpu.VMEM)
    anywhere = pl.BlockSpec(memory_space=pl.ANY)
    return pl.pallas_call(
        functools.partial(expert_kernel, count, down_tiles, hidden_tile),
        out_shape=[jax.ShapeDtypeStruct((rows, width), jnp.bfloat16)] * count,
        in_specs=[vmem] * (count + 1) + [anywhere] * 6,
        out_specs=[vmem] * count,
        scratch_shapes=[
            pltpu.VMEM((total, width), jnp.bfloat16),
            pltpu.VMEM((2, width, half), jnp.bfloat16),
            pltpu.VMEM((2, width, half), jnp.bfloat16),
            pltpu.VMEM((2, half, width), jnp.bfloat16),
            pltpu.VMEM((2, total, half), jnp.bfloat16),
            pltpu.SemaphoreType.DMA((4 * (half // hidden_tile) + 2 * down_tiles,)),
        ],
        compiler_params=pltpu.CompilerParams(vmem_limit_bytes=48 * 2**20),
        cost_estimate=pl.CostEstimate(
            flops=12 * total * width * half,
            bytes_accessed=12 * width * half + 4 * total * width,
            transcendentals=2 * total * half,
        ),
    )(*blocks, jnp.concatenate(scores, axis=0), *own, *other)


def added(*terms):
    return sum(term.astype(jnp.float32) for term in terms).astype(jnp.bfloat16)


def dense(tokens, expert_ids, gate_scores, gate_weight, up_weight, down_weight):
    node_count = lax.axis_size("node")
    local_count = lax.axis_size("local")
    node, local = lax.axis_index("node"), lax.axis_index("local")

    def next_node(value):
        pairs = [(source, (source + 1) % node_count) for source in range(node_count)]
        return lax.ppermute(value, "node", pairs)

    own = (gate_weight, up_weight, down_weight)
    other = tuple(partner(weight, "local", 0) for weight in own)

    experts = jnp.arange(node_count * (local_count // 2))
    named = expert_ids[:, :, None] == experts[None, None, :]
    factors = jnp.sum(jnp.where(named, gate_scores[:, :, None], 0), axis=1).astype(jnp.bfloat16)
    factors = lax.all_gather(factors, ("node", "local"))
    mine = node * (local_count // 2) + local // 2
    factors = lax.dynamic_index_in_dim(factors, mine, 2, keepdims=True).astype(jnp.float32)

    def factor_of(slot, here):
        source = lax.rem(node - slot + node_count, node_count) * local_count
        source += local if here else local ^ 2
        return lax.dynamic_index_in_dim(factors, source, 0, keepdims=False)

    along, across = [tokens], []
    for slot in range(node_count):
        across.append(partner(along[slot], "local", 1))
        if slot < node_count - 1:
            along.append(next_node(along[slot]))

    order = [("a", 0)]
    for slot in range(1, node_count):
        order += [("a", slot), ("x", slot - 1)]
    order.append(("x", node_count - 1))
    sizes = [3] + [2] * (node_count - 2) + [1]
    done = {}
    at = 0
    for size in sizes:
        keys = order[at : at + size]
        at += size
        blocks = [(along if kind == "a" else across)[slot] for kind, slot in keys]
        scores = [factor_of(slot, kind == "a") for kind, slot in keys]
        results = expert_rows(blocks, scores, own, other)
        done.update(zip(keys, results))

    running = None
    for slot in list(range(1, node_count)) + [0]:
        terms = [done["a", slot], partner(done["x", slot], "local", 1)]
        if running is not None:
            terms.append(running)
        running = added(*terms)
        if slot:
            running = next_node(running)
    return running


def body(tokens, expert_ids, gate_scores, gate_weight, up_weight, down_weight):
    per_group = lax.axis_size("local") // 2
    names_all = expert_ids.shape[1] == lax.axis_size("node") * per_group
    layer = dense if names_all and per_group == 2 else routed
    return layer(tokens, expert_ids, gate_scores, gate_weight, up_weight, down_weight)


def solution(mesh):
    in_specs = (
        P(("parts", "node", "local"), None),
        P(("parts", "node", "local"), None),
        P(("parts", "node", "local"), None),
        P(("node", "local"), None, None),
        P(("node", "local"), None, None),
        P(("node", "local"), None, None),
    )
    out_specs = P(("parts", "node", "local"), None)
    return jax.shard_map(body, mesh=mesh, in_specs=in_specs, out_specs=out_specs, check_vma=False)
```

```python
import functools

import jax
import jax.numpy as jnp
from jax import lax
from jax.experimental import pallas as pl
from jax.experimental.pallas import tpu as pltpu
from jax.sharding import PartitionSpec as P

TOPG = 4


def partner(value, axis, bit):
    mask = 2**bit
    pairs = [(source, source ^ mask) for source in range(lax.axis_size(axis))]
    return lax.ppermute(value, axis, pairs)


def expert_apply(arrived, gate_weight, up_weight, down_weight):
    layout = arrived.shape
    flat_rows = arrived.reshape(-1, layout[-1])
    gate_act = jnp.dot(flat_rows, gate_weight[0], preferred_element_type=jnp.float32)
    up_act = jnp.dot(flat_rows, up_weight[0], preferred_element_type=jnp.float32)
    hidden = (jax.nn.silu(gate_act) * up_act).astype(jnp.bfloat16)
    result = jnp.dot(hidden, down_weight[0], preferred_element_type=jnp.float32).astype(
        jnp.bfloat16
    )
    return result.reshape(layout)


def routed(tokens, expert_ids, gate_scores, gate_weight, up_weight, down_weight):
    rows_dev, model_width = tokens.shape
    node_count = lax.axis_size("node")
    local_count = lax.axis_size("local")
    per_group = local_count // 2
    chooser_cap = rows_dev * TOPG // node_count
    bound_most = min(chooser_cap, 3 * chooser_cap // per_group)
    group_ids = jnp.arange(node_count)
    owner_group = expert_ids // per_group
    chosen = jnp.any(owner_group[:, :, None] == group_ids[None, None, :], axis=1)
    chosen_int = chosen.astype(jnp.int32)
    before = jnp.cumsum(chosen_int, axis=0) - chosen_int
    select_one = chosen.T[:, None, :] & (
        before.T[:, None, :] == jnp.arange(chooser_cap)[None, :, None]
    )
    one_hot = select_one.astype(jnp.bfloat16)
    send_rows = jnp.einsum(
        "gsb,bd->gsd", one_hot, tokens, preferred_element_type=jnp.float32
    ).astype(jnp.bfloat16)
    token_at = jnp.sum(jnp.where(select_one, jnp.arange(rows_dev)[None, None, :], 0), axis=-1)
    occupied = jnp.any(select_one, axis=-1)
    inside = (owner_group[token_at] == group_ids[:, None, None]) & occupied[:, :, None]
    send_ids = jnp.where(inside, expert_ids[token_at] % per_group, -1)
    send_scores = jnp.where(inside, gate_scores[token_at], 0)
    arrived_rows, arrived_ids, arrived_scores = (
        lax.all_to_all(send_rows, "node", split_axis=0, concat_axis=0, tiled=True),
        lax.all_to_all(send_ids, "node", split_axis=0, concat_axis=0, tiled=True),
        lax.all_to_all(send_scores, "node", split_axis=0, concat_axis=0, tiled=True),
    )
    relayed = node_count * chooser_cap
    relay_rows = arrived_rows.reshape(relayed, model_width)
    relay_ids = arrived_ids.reshape(relayed, -1)
    relay_scores = arrived_scores.reshape(relayed, -1).astype(jnp.float32)
    member_ids = jnp.arange(per_group)
    matches = relay_ids[:, :, None] == member_ids[None, None, :]
    naming = jnp.any(matches, axis=1)
    naming_int = naming.astype(jnp.int32)
    ahead_count = jnp.cumsum(naming_int, axis=0) - naming_int
    group_cap = node_count * bound_most
    half_cap = group_cap // 2
    select_two = naming.T[:, None, :] & (
        ahead_count.T[:, None, :] == jnp.arange(group_cap)[None, :, None]
    )
    expert_rows = jnp.einsum(
        "jsr,rd->jsd",
        select_two.astype(jnp.bfloat16),
        relay_rows,
        preferred_element_type=jnp.float32,
    ).astype(jnp.bfloat16)
    outbound = expert_rows.reshape(local_count, half_cap, model_width)
    arrived = lax.all_to_all(outbound, "local", split_axis=0, concat_axis=0, tiled=True)
    partner_rows = partner(arrived, "local", 0)
    stacked = jnp.concatenate([arrived, partner_rows], axis=0)
    outputs = expert_apply(stacked, gate_weight, up_weight, down_weight)
    count = arrived.shape[0]
    mine = outputs[:count]
    theirs = outputs[count:]
    back = partner(theirs, "local", 0)
    partials = (mine.astype(jnp.float32) + back.astype(jnp.float32)).astype(jnp.bfloat16)
    returned = lax.all_to_all(partials, "local", split_axis=0, concat_axis=0, tiled=True)
    relay_weight = jnp.sum(jnp.where(matches, relay_scores[:, :, None], 0.0), axis=1)
    weighted = (jnp.transpose(select_two, (2, 0, 1)) * relay_weight[:, :, None]).astype(
        jnp.bfloat16
    )
    expert_output = returned.reshape(per_group, group_cap, model_width)
    group_sum = jnp.einsum(
        "rjs,jsd->rd", weighted, expert_output, preferred_element_type=jnp.float32
    ).astype(jnp.bfloat16)
    gathered_back = lax.all_to_all(
        group_sum.reshape(node_count, chooser_cap, model_width),
        "node",
        split_axis=0,
        concat_axis=0,
        tiled=True,
    )
    combined = jnp.einsum("gsb,gsd->bd", one_hot, gathered_back, preferred_element_type=jnp.float32)
    return combined.astype(jnp.bfloat16)

def expert_kernel(counts, down_tiles, hidden_tile, *refs):
    taken, given = counts
    blocks, scores, weights = refs[:taken], refs[taken], refs[taken + 1 : taken + 7]
    outs = refs[taken + 7 : taken + 7 + given]
    rows_all, gate, up, down, hidden, sems = refs[taken + 7 + given :]
    width = rows_all.shape[1]
    half = gate.shape[-1]
    started = []

    def fetch(source, target):
        copy = pltpu.make_async_copy(source, target, sems.at[len(started)])
        copy.start()
        started.append(copy)
        return copy

    first, second = [], []
    for side in range(2):
        gate_hbm, up_hbm, _ = weights[3 * side : 3 * side + 3]
        for start in range(0, half, hidden_tile):
            cols = pl.ds(start, hidden_tile)
            pair = (
                fetch(gate_hbm.at[0, :, cols], gate.at[side, :, cols]),
                fetch(up_hbm.at[0, :, cols], up.at[side, :, cols]),
            )
            first.append((side, cols, pair))
    step = width // down_tiles
    for start in range(0, width, step):
        cols = pl.ds(start, step)
        pair = tuple(
            fetch(weights[3 * side + 2].at[0, :, cols], down.at[side, :, cols]) for side in range(2)
        )
        second.append((cols, pair))
    at = 0
    for block in blocks:
        rows_all[pl.ds(at, block.shape[0]), :] = block[...]
        at += block.shape[0]
    for side, cols, pair in first:
        for copy in pair:
            copy.wait()
        gate_act = jnp.dot(rows_all[...], gate[side, :, cols], preferred_element_type=jnp.float32)
        up_act = jnp.dot(rows_all[...], up[side, :, cols], preferred_element_type=jnp.float32)
        hidden[side, :, cols] = (jax.nn.silu(gate_act) * up_act).astype(jnp.bfloat16)
    for cols, pair in second:
        for copy in pair:
            copy.wait()
        result = jnp.dot(hidden[0], down[0, :, cols], preferred_element_type=jnp.float32)
        result += jnp.dot(hidden[1], down[1, :, cols], preferred_element_type=jnp.float32)
        result = (result * scores[...]).astype(jnp.bfloat16)
        at = 0
        for out in outs:
            out[:, cols] = result[at : at + out.shape[0]]
            at += out.shape[0]


def expert_rows(blocks, scores, own, other, out_rows):
    width = blocks[0].shape[1]
    half = own[0].shape[-1]
    total = sum(block.shape[0] for block in blocks)
    given = total // out_rows
    down_tiles = 4
    hidden_tile = half // 2
    vmem = pl.BlockSpec(memory_space=pltpu.VMEM)
    anywhere = pl.BlockSpec(memory_space=pl.ANY)
    return pl.pallas_call(
        functools.partial(expert_kernel, (len(blocks), given), down_tiles, hidden_tile),
        out_shape=[jax.ShapeDtypeStruct((out_rows, width), jnp.bfloat16)] * given,
        in_specs=[vmem] * (len(blocks) + 1) + [anywhere] * 6,
        out_specs=[vmem] * given,
        scratch_shapes=[
            pltpu.VMEM((total, width), jnp.bfloat16),
            pltpu.VMEM((2, width, half), jnp.bfloat16),
            pltpu.VMEM((2, width, half), jnp.bfloat16),
            pltpu.VMEM((2, half, width), jnp.bfloat16),
            pltpu.VMEM((2, total, half), jnp.bfloat16),
            pltpu.SemaphoreType.DMA((4 * (half // hidden_tile) + 2 * down_tiles,)),
        ],
        compiler_params=pltpu.CompilerParams(vmem_limit_bytes=48 * 2**20),
        cost_estimate=pl.CostEstimate(
            flops=12 * total * width * half,
            bytes_accessed=12 * width * half + 4 * total * width,
            transcendentals=2 * total * half,
        ),
    )(*blocks, scores, *own, *other)


def added(*terms):
    return sum(term.astype(jnp.float32) for term in terms).astype(jnp.bfloat16)


def together(*values):
    return lax.optimization_barrier(values)


def dense(tokens, expert_ids, gate_scores, gate_weight, up_weight, down_weight):
    node_count = lax.axis_size("node")
    local_count = lax.axis_size("local")
    node, local = lax.axis_index("node"), lax.axis_index("local")
    rows = tokens.shape[0]
    split = rows // 2
    last = node_count - 1

    def next_node(value):
        pairs = [(source, (source + 1) % node_count) for source in range(node_count)]
        return lax.ppermute(value, "node", pairs)

    def other_x(value):
        return partner(value, "local", 1)

    own = (gate_weight, up_weight, down_weight)
    other = tuple(partner(weight, "local", 0) for weight in own)

    experts = jnp.arange(node_count * (local_count // 2))
    named = expert_ids[:, :, None] == experts[None, None, :]
    factors = jnp.sum(jnp.where(named, gate_scores[:, :, None], 0), axis=1).astype(jnp.bfloat16)
    factors = jnp.stack([factors, other_x(factors)])
    bit = 0
    while 2**bit < node_count:
        factors = jnp.concatenate([factors, partner(factors, "node", bit)])
        bit += 1
    mine = node * (local_count // 2) + local // 2
    factors = lax.dynamic_index_in_dim(factors, mine, 2, keepdims=True).astype(jnp.float32)

    def factor_of(kind, slot):
        source = lax.rem(node - slot + node_count, node_count)
        at = 2 * (source ^ node) + (0 if kind == "a" else 1)
        return lax.dynamic_index_in_dim(factors, at, 0, keepdims=False)

    done = {}

    def work(keys, parts=None):
        blocks = parts or [(along if kind == "a" else across)[slot] for kind, slot in keys]
        scores = jnp.concatenate([factor_of(*key) for key in keys])
        results = expert_rows(blocks, scores, own, other, rows)
        done.update(zip(keys, results))
        return results

    def hold(keys, *values):
        held = together(*values, *[done[key] for key in keys])
        done.update(zip(keys, held[len(values) :]))
        return held[: len(values)]

    along, across = [tokens], []
    early = [("a", 0)] + [(kind, slot) for slot in range(1, last) for kind in "ax"]
    early = [("a", 0)]
    for slot in range(1, last):
        early += [("a", slot), ("x", slot - 1)]
    for slot in range(last):
        moved, crossed = next_node(along[slot]), other_x(along[slot])
        if slot < last - 1:
            moved, crossed = together(moved, crossed)
        else:
            work(early)
            moved, crossed = hold(early, moved, crossed)
        along.append(moved)
        across.append(crossed)
    upper, lower = other_x(along[last][:split]), next_node(across[last - 1][split:])
    middle = [("a", last), ("x", last - 1)]
    work(middle)
    upper, lower = hold(middle, upper, lower)

    crossed, passed = together(other_x(done["x", 1][:split]), next_node(done["x", 1][split:]))
    second = done["x", 2]
    done["x", 2] = jnp.concatenate([second[:split], added(second[split:], passed)])
    first = done["a", 1]
    running = jnp.concatenate([added(first[:split], crossed), first[split:]])
    for slot in list(range(2, node_count)) + [0]:
        crossed, moved = other_x(done["x", slot]), next_node(running)
        if slot == 2:
            late = [("x", last)]
            work(late, [upper, lower])
            crossed, moved = hold(late, crossed, moved)
        elif slot:
            crossed, moved = together(crossed, moved)
        running = added(done["a", slot], crossed, moved)
    return running


def body(tokens, expert_ids, gate_scores, gate_weight, up_weight, down_weight):
    per_group = lax.axis_size("local") // 2
    names_all = expert_ids.shape[1] == lax.axis_size("node") * per_group
    layer = dense if names_all and per_group == 2 else routed
    return layer(tokens, expert_ids, gate_scores, gate_weight, up_weight, down_weight)


def solution(mesh):
    in_specs = (
        P(("parts", "node", "local"), None),
        P(("parts", "node", "local"), None),
        P(("parts", "node", "local"), None),
        P(("node", "local"), None, None),
        P(("node", "local"), None, None),
        P(("node", "local"), None, None),
    )
    out_specs = P(("parts", "node", "local"), None)
    return jax.shard_map(body, mesh=mesh, in_specs=in_specs, out_specs=out_specs, check_vma=False)
```

```python
import functools

import jax
import jax.numpy as jnp
from jax import lax
from jax.experimental import pallas as pl
from jax.experimental.pallas import tpu as pltpu
from jax.sharding import PartitionSpec as P

TOPG = 4


def partner(value, axis, bit):
    mask = 2**bit
    pairs = [(source, source ^ mask) for source in range(lax.axis_size(axis))]
    return lax.ppermute(value, axis, pairs)


def expert_apply(arrived, gate_weight, up_weight, down_weight):
    layout = arrived.shape
    flat_rows = arrived.reshape(-1, layout[-1])
    gate_act = jnp.dot(flat_rows, gate_weight[0], preferred_element_type=jnp.float32)
    up_act = jnp.dot(flat_rows, up_weight[0], preferred_element_type=jnp.float32)
    hidden = (jax.nn.silu(gate_act) * up_act).astype(jnp.bfloat16)
    result = jnp.dot(hidden, down_weight[0], preferred_element_type=jnp.float32).astype(
        jnp.bfloat16
    )
    return result.reshape(layout)


def routed(tokens, expert_ids, gate_scores, gate_weight, up_weight, down_weight):
    rows_dev, model_width = tokens.shape
    node_count = lax.axis_size("node")
    local_count = lax.axis_size("local")
    per_group = local_count // 2
    chooser_cap = rows_dev * TOPG // node_count
    bound_most = min(chooser_cap, 3 * chooser_cap // per_group)
    group_ids = jnp.arange(node_count)
    owner_group = expert_ids // per_group
    chosen = jnp.any(owner_group[:, :, None] == group_ids[None, None, :], axis=1)
    chosen_int = chosen.astype(jnp.int32)
    before = jnp.cumsum(chosen_int, axis=0) - chosen_int
    select_one = chosen.T[:, None, :] & (
        before.T[:, None, :] == jnp.arange(chooser_cap)[None, :, None]
    )
    one_hot = select_one.astype(jnp.bfloat16)
    send_rows = jnp.einsum(
        "gsb,bd->gsd", one_hot, tokens, preferred_element_type=jnp.float32
    ).astype(jnp.bfloat16)
    token_at = jnp.sum(jnp.where(select_one, jnp.arange(rows_dev)[None, None, :], 0), axis=-1)
    occupied = jnp.any(select_one, axis=-1)
    inside = (owner_group[token_at] == group_ids[:, None, None]) & occupied[:, :, None]
    send_ids = jnp.where(inside, expert_ids[token_at] % per_group, -1)
    send_scores = jnp.where(inside, gate_scores[token_at], 0)
    arrived_rows, arrived_ids, arrived_scores = (
        lax.all_to_all(send_rows, "node", split_axis=0, concat_axis=0, tiled=True),
        lax.all_to_all(send_ids, "node", split_axis=0, concat_axis=0, tiled=True),
        lax.all_to_all(send_scores, "node", split_axis=0, concat_axis=0, tiled=True),
    )
    relayed = node_count * chooser_cap
    relay_rows = arrived_rows.reshape(relayed, model_width)
    relay_ids = arrived_ids.reshape(relayed, -1)
    relay_scores = arrived_scores.reshape(relayed, -1).astype(jnp.float32)
    member_ids = jnp.arange(per_group)
    matches = relay_ids[:, :, None] == member_ids[None, None, :]
    naming = jnp.any(matches, axis=1)
    naming_int = naming.astype(jnp.int32)
    ahead_count = jnp.cumsum(naming_int, axis=0) - naming_int
    group_cap = node_count * bound_most
    half_cap = group_cap // 2
    select_two = naming.T[:, None, :] & (
        ahead_count.T[:, None, :] == jnp.arange(group_cap)[None, :, None]
    )
    expert_rows = jnp.einsum(
        "jsr,rd->jsd",
        select_two.astype(jnp.bfloat16),
        relay_rows,
        preferred_element_type=jnp.float32,
    ).astype(jnp.bfloat16)
    outbound = expert_rows.reshape(local_count, half_cap, model_width)
    arrived = lax.all_to_all(outbound, "local", split_axis=0, concat_axis=0, tiled=True)
    partner_rows = partner(arrived, "local", 0)
    stacked = jnp.concatenate([arrived, partner_rows], axis=0)
    outputs = expert_apply(stacked, gate_weight, up_weight, down_weight)
    count = arrived.shape[0]
    mine = outputs[:count]
    theirs = outputs[count:]
    back = partner(theirs, "local", 0)
    partials = (mine.astype(jnp.float32) + back.astype(jnp.float32)).astype(jnp.bfloat16)
    returned = lax.all_to_all(partials, "local", split_axis=0, concat_axis=0, tiled=True)
    relay_weight = jnp.sum(jnp.where(matches, relay_scores[:, :, None], 0.0), axis=1)
    weighted = (jnp.transpose(select_two, (2, 0, 1)) * relay_weight[:, :, None]).astype(
        jnp.bfloat16
    )
    expert_output = returned.reshape(per_group, group_cap, model_width)
    group_sum = jnp.einsum(
        "rjs,jsd->rd", weighted, expert_output, preferred_element_type=jnp.float32
    ).astype(jnp.bfloat16)
    gathered_back = lax.all_to_all(
        group_sum.reshape(node_count, chooser_cap, model_width),
        "node",
        split_axis=0,
        concat_axis=0,
        tiled=True,
    )
    combined = jnp.einsum("gsb,gsd->bd", one_hot, gathered_back, preferred_element_type=jnp.float32)
    return combined.astype(jnp.bfloat16)

LANES = 128


def pack_kernel(tokens, expert_ids, gate_scores, *packed):
    rows, width = tokens.shape
    lane = lax.broadcasted_iota(jnp.int32, (LANES, rows), 0)
    found = jnp.zeros((LANES, rows), jnp.float32)
    for k in range(expert_ids.shape[0]):
        score = gate_scores[k : k + 1, :].astype(jnp.float32)
        found += jnp.where(lane == expert_ids[k : k + 1, :], score, 0.0)
    factors = found.T.astype(jnp.bfloat16)
    at = 0
    for out in packed:
        piece = out.shape[0]
        out[:, :width] = tokens[at : at + piece, :]
        out[:, width:] = factors[at : at + piece]
        at += piece


def pack(tokens, expert_ids, gate_scores, pieces):
    rows, width = tokens.shape
    vmem = pl.BlockSpec(memory_space=pltpu.VMEM)
    shape = jax.ShapeDtypeStruct((rows // pieces, width + LANES), tokens.dtype)
    return pl.pallas_call(
        pack_kernel,
        out_shape=[shape] * pieces,
        in_specs=[vmem] * 3,
        out_specs=[vmem] * pieces,
    )(tokens, expert_ids.T, gate_scores.T)


def expert_kernel(taken, down_tiles, hidden_tile, mine, *refs):
    blocks, weights, outs = refs[:taken], refs[taken : taken + 6], refs[taken + 6 : -6]
    rows_all, gate, up, down, hidden, sems = refs[-6:]
    width = down.shape[2]
    half = gate.shape[2]
    started = []

    def fetch(source, target):
        copy = pltpu.make_async_copy(source, target, sems.at[len(started)])
        copy.start()
        started.append(copy)
        return copy

    first, second = [], []
    for side in range(2):
        gate_hbm, up_hbm, _ = weights[3 * side : 3 * side + 3]
        for start in range(0, half, hidden_tile):
            cols = pl.ds(start, hidden_tile)
            pair = (
                fetch(gate_hbm.at[0, :, cols], gate.at[side, :, cols]),
                fetch(up_hbm.at[0, :, cols], up.at[side, :, cols]),
            )
            first.append((side, cols, pair))
    step = width // down_tiles
    for start in range(0, width, step):
        cols = pl.ds(start, step)
        pair = tuple(
            fetch(weights[3 * side + 2].at[0, :, cols], down.at[side, :, cols]) for side in range(2)
        )
        second.append((cols, pair))
    at = 0
    for block in blocks:
        rows_all[pl.ds(at, block.shape[0]), :] = block[...]
        at += block.shape[0]
    lane = lax.broadcasted_iota(jnp.int32, (at, LANES), 1)
    factors = rows_all[:, width:].astype(jnp.float32)
    factor = jnp.sum(jnp.where(lane == mine[0], factors, 0.0), axis=1, keepdims=True)
    for side, cols, pair in first:
        for copy in pair:
            copy.wait()
        rows = rows_all[:, :width]
        gate_act = jnp.dot(rows, gate[side, :, cols], preferred_element_type=jnp.float32)
        up_act = jnp.dot(rows, up[side, :, cols], preferred_element_type=jnp.float32)
        hidden[side, :, cols] = (jax.nn.silu(gate_act) * up_act).astype(jnp.bfloat16)
    for cols, pair in second:
        for copy in pair:
            copy.wait()
        result = jnp.dot(hidden[0], down[0, :, cols], preferred_element_type=jnp.float32)
        result += jnp.dot(hidden[1], down[1, :, cols], preferred_element_type=jnp.float32)
        result = (result * factor).astype(jnp.bfloat16)
        at = 0
        for out in outs:
            out[:, cols] = result[at : at + out.shape[0]]
            at += out.shape[0]


def expert_rows(blocks, mine, own, other, out_rows):
    half, width = own[2].shape[1:]
    total = sum(block.shape[0] for block in blocks)
    down_tiles = 4
    hidden_tile = half // 2
    vmem = pl.BlockSpec(memory_space=pltpu.VMEM)
    anywhere = pl.BlockSpec(memory_space=pl.ANY)
    return pl.pallas_call(
        functools.partial(expert_kernel, len(blocks), down_tiles, hidden_tile),
        out_shape=[jax.ShapeDtypeStruct((rows, width), jnp.bfloat16) for rows in out_rows],
        in_specs=[pl.BlockSpec(memory_space=pltpu.SMEM)] + [vmem] * len(blocks) + [anywhere] * 6,
        out_specs=[vmem] * len(out_rows),
        scratch_shapes=[
            pltpu.VMEM((total, width + LANES), jnp.bfloat16),
            pltpu.VMEM((2, width, half), jnp.bfloat16),
            pltpu.VMEM((2, width, half), jnp.bfloat16),
            pltpu.VMEM((2, half, width), jnp.bfloat16),
            pltpu.VMEM((2, total, half), jnp.bfloat16),
            pltpu.SemaphoreType.DMA((4 * (half // hidden_tile) + 2 * down_tiles,)),
        ],
        compiler_params=pltpu.CompilerParams(vmem_limit_bytes=48 * 2**20),
        cost_estimate=pl.CostEstimate(
            flops=12 * total * width * half,
            bytes_accessed=12 * width * half + 4 * total * width,
            transcendentals=2 * total * half,
        ),
    )(mine, *blocks, *own, *other)


def added(*terms):
    return sum(term.astype(jnp.float32) for term in terms).astype(jnp.bfloat16)


def together(*values):
    return lax.optimization_barrier(values)


def after(value, *others):
    for other in others:
        same = other if other.shape == value.shape else other[:, :1]
        value = jnp.where(same == same, value, same)
    return value


def dense(tokens, expert_ids, gate_scores, gate_weight, up_weight, down_weight):
    node_count = lax.axis_size("node")
    local_count = lax.axis_size("local")
    rows = tokens.shape[0]
    split = rows // 2
    last = node_count - 1

    def next_node(value):
        pairs = [(source, (source + 1) % node_count) for source in range(node_count)]
        return lax.ppermute(value, "node", pairs)

    def other_x(value):
        return partner(value, "local", 1)

    mine = lax.axis_index("node") * (local_count // 2) + lax.axis_index("local") // 2
    mine = jnp.full((1,), mine, jnp.int32)
    own = (gate_weight, up_weight, down_weight)
    other = tuple(partner(weight, "local", 0) for weight in own)

    along, across = list(pack(tokens, expert_ids, gate_scores, 1)), []
    for slot in range(last):
        crossed, moved = other_x(along[slot]), next_node(along[slot])
        if slot < last - 1:
            moved = after(moved, crossed)
        along.append(moved)
        across.append(crossed)
    early = along[:last] + across[: last - 1]
    sizes = [rows] * last + [rows, split, split] + [rows] * (last - 3)
    results = list(expert_rows(early, mine, own, other, sizes))
    at_home, away = results[:last], [results[last], None] + results[last + 3 :]
    first_upper, first_lower = results[last + 1 : last + 3]
    upper = other_x(after(along[last][:split], first_upper))
    lower = next_node(after(across[last - 1][split:], first_lower))
    middle = expert_rows([along[last], across[last - 1]], mine, own, other, [rows, rows])
    at_home.append(middle[0])

    crossed, passed = other_x(first_upper), next_node(first_lower)
    second = [after(middle[1][:split], upper, lower), added(middle[1][split:], passed)]
    away.append(jnp.concatenate(second))
    away += expert_rows([upper, lower], mine, own, other, [rows])
    first = at_home[1]
    running = jnp.concatenate([added(first[:split], crossed), first[split:]])
    for slot in list(range(2, node_count)) + [0]:
        crossed, moved = other_x(away[slot]), next_node(running)
        running = added(at_home[slot], crossed, moved)
        if slot:
            following = (slot + 1) % node_count
            away[following] = after(away[following], crossed)
    return running


def body(tokens, expert_ids, gate_scores, gate_weight, up_weight, down_weight):
    per_group = lax.axis_size("local") // 2
    names_all = expert_ids.shape[1] == lax.axis_size("node") * per_group
    layer = dense if names_all and per_group == 2 else routed
    return layer(tokens, expert_ids, gate_scores, gate_weight, up_weight, down_weight)


def solution(mesh):
    in_specs = (
        P(("parts", "node", "local"), None),
        P(("parts", "node", "local"), None),
        P(("parts", "node", "local"), None),
        P(("node", "local"), None, None),
        P(("node", "local"), None, None),
        P(("node", "local"), None, None),
    )
    out_specs = P(("parts", "node", "local"), None)
    return jax.shard_map(body, mesh=mesh, in_specs=in_specs, out_specs=out_specs, check_vma=False)
```

```python
import functools

import jax
import jax.numpy as jnp
from jax import lax
from jax.experimental import pallas as pl
from jax.experimental.pallas import tpu as pltpu
from jax.sharding import PartitionSpec as P

TOPG = 4


def partner(value, axis, bit):
    mask = 2**bit
    pairs = [(source, source ^ mask) for source in range(lax.axis_size(axis))]
    return lax.ppermute(value, axis, pairs)


def expert_apply(arrived, gate_weight, up_weight, down_weight):
    layout = arrived.shape
    flat_rows = arrived.reshape(-1, layout[-1])
    gate_act = jnp.dot(flat_rows, gate_weight[0], preferred_element_type=jnp.float32)
    up_act = jnp.dot(flat_rows, up_weight[0], preferred_element_type=jnp.float32)
    hidden = (jax.nn.silu(gate_act) * up_act).astype(jnp.bfloat16)
    result = jnp.dot(hidden, down_weight[0], preferred_element_type=jnp.float32).astype(
        jnp.bfloat16
    )
    return result.reshape(layout)


def routed(tokens, expert_ids, gate_scores, gate_weight, up_weight, down_weight):
    rows_dev, model_width = tokens.shape
    node_count = lax.axis_size("node")
    local_count = lax.axis_size("local")
    per_group = local_count // 2
    chooser_cap = rows_dev * TOPG // node_count
    bound_most = min(chooser_cap, 3 * chooser_cap // per_group)
    group_ids = jnp.arange(node_count)
    owner_group = expert_ids // per_group
    chosen = jnp.any(owner_group[:, :, None] == group_ids[None, None, :], axis=1)
    chosen_int = chosen.astype(jnp.int32)
    before = jnp.cumsum(chosen_int, axis=0) - chosen_int
    select_one = chosen.T[:, None, :] & (
        before.T[:, None, :] == jnp.arange(chooser_cap)[None, :, None]
    )
    one_hot = select_one.astype(jnp.bfloat16)
    send_rows = jnp.einsum(
        "gsb,bd->gsd", one_hot, tokens, preferred_element_type=jnp.float32
    ).astype(jnp.bfloat16)
    token_at = jnp.sum(jnp.where(select_one, jnp.arange(rows_dev)[None, None, :], 0), axis=-1)
    occupied = jnp.any(select_one, axis=-1)
    inside = (owner_group[token_at] == group_ids[:, None, None]) & occupied[:, :, None]
    send_ids = jnp.where(inside, expert_ids[token_at] % per_group, -1)
    send_scores = jnp.where(inside, gate_scores[token_at], 0)
    arrived_rows, arrived_ids, arrived_scores = (
        lax.all_to_all(send_rows, "node", split_axis=0, concat_axis=0, tiled=True),
        lax.all_to_all(send_ids, "node", split_axis=0, concat_axis=0, tiled=True),
        lax.all_to_all(send_scores, "node", split_axis=0, concat_axis=0, tiled=True),
    )
    relayed = node_count * chooser_cap
    relay_rows = arrived_rows.reshape(relayed, model_width)
    relay_ids = arrived_ids.reshape(relayed, -1)
    relay_scores = arrived_scores.reshape(relayed, -1).astype(jnp.float32)
    member_ids = jnp.arange(per_group)
    matches = relay_ids[:, :, None] == member_ids[None, None, :]
    naming = jnp.any(matches, axis=1)
    naming_int = naming.astype(jnp.int32)
    ahead_count = jnp.cumsum(naming_int, axis=0) - naming_int
    group_cap = node_count * bound_most
    half_cap = group_cap // 2
    select_two = naming.T[:, None, :] & (
        ahead_count.T[:, None, :] == jnp.arange(group_cap)[None, :, None]
    )
    expert_rows = jnp.einsum(
        "jsr,rd->jsd",
        select_two.astype(jnp.bfloat16),
        relay_rows,
        preferred_element_type=jnp.float32,
    ).astype(jnp.bfloat16)
    outbound = expert_rows.reshape(local_count, half_cap, model_width)
    arrived = lax.all_to_all(outbound, "local", split_axis=0, concat_axis=0, tiled=True)
    partner_rows = partner(arrived, "local", 0)
    stacked = jnp.concatenate([arrived, partner_rows], axis=0)
    outputs = expert_apply(stacked, gate_weight, up_weight, down_weight)
    count = arrived.shape[0]
    mine = outputs[:count]
    theirs = outputs[count:]
    back = partner(theirs, "local", 0)
    partials = (mine.astype(jnp.float32) + back.astype(jnp.float32)).astype(jnp.bfloat16)
    returned = lax.all_to_all(partials, "local", split_axis=0, concat_axis=0, tiled=True)
    relay_weight = jnp.sum(jnp.where(matches, relay_scores[:, :, None], 0.0), axis=1)
    weighted = (jnp.transpose(select_two, (2, 0, 1)) * relay_weight[:, :, None]).astype(
        jnp.bfloat16
    )
    expert_output = returned.reshape(per_group, group_cap, model_width)
    group_sum = jnp.einsum(
        "rjs,jsd->rd", weighted, expert_output, preferred_element_type=jnp.float32
    ).astype(jnp.bfloat16)
    gathered_back = lax.all_to_all(
        group_sum.reshape(node_count, chooser_cap, model_width),
        "node",
        split_axis=0,
        concat_axis=0,
        tiled=True,
    )
    combined = jnp.einsum("gsb,gsd->bd", one_hot, gathered_back, preferred_element_type=jnp.float32)
    return combined.astype(jnp.bfloat16)

LANES = 128


def pack_kernel(tokens, expert_ids, gate_scores, *packed):
    rows, width = tokens.shape
    lane = lax.broadcasted_iota(jnp.int32, (LANES, rows), 0)
    found = jnp.zeros((LANES, rows), jnp.float32)
    for k in range(expert_ids.shape[0]):
        score = gate_scores[k : k + 1, :].astype(jnp.float32)
        found += jnp.where(lane == expert_ids[k : k + 1, :], score, 0.0)
    factors = found.T.astype(jnp.bfloat16)
    at = 0
    for out in packed:
        piece = out.shape[0]
        out[:, :width] = tokens[at : at + piece, :]
        out[:, width:] = factors[at : at + piece]
        at += piece


def pack(tokens, expert_ids, gate_scores, pieces):
    rows, width = tokens.shape
    vmem = pl.BlockSpec(memory_space=pltpu.VMEM)
    shape = jax.ShapeDtypeStruct((rows // pieces, width + LANES), tokens.dtype)
    return pl.pallas_call(
        pack_kernel,
        out_shape=[shape] * pieces,
        in_specs=[vmem] * 3,
        out_specs=[vmem] * pieces,
    )(tokens, expert_ids.T, gate_scores.T)


def expert_kernel(taken, down_tiles, hidden_tile, mine, *refs):
    blocks, weights, outs = refs[:taken], refs[taken : taken + 6], refs[taken + 6 : -6]
    rows_all, gate, up, down, hidden, sems = refs[-6:]
    width = down.shape[2]
    half = gate.shape[2]
    started = []

    def fetch(source, target):
        copy = pltpu.make_async_copy(source, target, sems.at[len(started)])
        copy.start()
        started.append(copy)
        return copy

    first, second = [], []
    for side in range(2):
        gate_hbm, up_hbm, _ = weights[3 * side : 3 * side + 3]
        for start in range(0, half, hidden_tile):
            cols = pl.ds(start, hidden_tile)
            pair = (
                fetch(gate_hbm.at[0, :, cols], gate.at[side, :, cols]),
                fetch(up_hbm.at[0, :, cols], up.at[side, :, cols]),
            )
            first.append((side, cols, pair))
    step = width // down_tiles
    for start in range(0, width, step):
        cols = pl.ds(start, step)
        pair = tuple(
            fetch(weights[3 * side + 2].at[0, :, cols], down.at[side, :, cols]) for side in range(2)
        )
        second.append((cols, pair))
    at = 0
    for block in blocks:
        rows_all[pl.ds(at, block.shape[0]), :] = block[...]
        at += block.shape[0]
    lane = lax.broadcasted_iota(jnp.int32, (at, LANES), 1)
    factors = rows_all[:, width:].astype(jnp.float32)
    factor = jnp.sum(jnp.where(lane == mine[0], factors, 0.0), axis=1, keepdims=True)
    for side, cols, pair in first:
        for copy in pair:
            copy.wait()
        rows = rows_all[:, :width]
        gate_act = jnp.dot(rows, gate[side, :, cols], preferred_element_type=jnp.float32)
        up_act = jnp.dot(rows, up[side, :, cols], preferred_element_type=jnp.float32)
        hidden[side, :, cols] = (jax.nn.silu(gate_act) * up_act).astype(jnp.bfloat16)
    for cols, pair in second:
        for copy in pair:
            copy.wait()
        result = jnp.dot(hidden[0], down[0, :, cols], preferred_element_type=jnp.float32)
        result += jnp.dot(hidden[1], down[1, :, cols], preferred_element_type=jnp.float32)
        result = (result * factor).astype(jnp.bfloat16)
        at = 0
        for out in outs:
            out[:, cols] = result[at : at + out.shape[0]]
            at += out.shape[0]


def expert_rows(blocks, mine, own, other, out_rows):
    half, width = own[2].shape[1:]
    total = sum(block.shape[0] for block in blocks)
    down_tiles = 4
    hidden_tile = half // 2
    vmem = pl.BlockSpec(memory_space=pltpu.VMEM)
    anywhere = pl.BlockSpec(memory_space=pl.ANY)
    return pl.pallas_call(
        functools.partial(expert_kernel, len(blocks), down_tiles, hidden_tile),
        out_shape=[jax.ShapeDtypeStruct((rows, width), jnp.bfloat16) for rows in out_rows],
        in_specs=[pl.BlockSpec(memory_space=pltpu.SMEM)] + [vmem] * len(blocks) + [anywhere] * 6,
        out_specs=[vmem] * len(out_rows),
        scratch_shapes=[
            pltpu.VMEM((total, width + LANES), jnp.bfloat16),
            pltpu.VMEM((2, width, half), jnp.bfloat16),
            pltpu.VMEM((2, width, half), jnp.bfloat16),
            pltpu.VMEM((2, half, width), jnp.bfloat16),
            pltpu.VMEM((2, total, half), jnp.bfloat16),
            pltpu.SemaphoreType.DMA((4 * (half // hidden_tile) + 2 * down_tiles,)),
        ],
        compiler_params=pltpu.CompilerParams(vmem_limit_bytes=48 * 2**20),
        cost_estimate=pl.CostEstimate(
            flops=12 * total * width * half,
            bytes_accessed=12 * width * half + 4 * total * width,
            transcendentals=2 * total * half,
        ),
    )(mine, *blocks, *own, *other)


def added(*terms):
    return sum(term.astype(jnp.float32) for term in terms).astype(jnp.bfloat16)


def together(*values):
    return lax.optimization_barrier(values)


def after(value, *others):
    for other in others:
        same = other if other.shape == value.shape else other[:, :1]
        value = jnp.where(same == same, value, same)
    return value


def dense(tokens, expert_ids, gate_scores, gate_weight, up_weight, down_weight):
    node_count = lax.axis_size("node")
    local_count = lax.axis_size("local")
    rows = tokens.shape[0]
    split = rows // 2
    last = node_count - 1

    ring = list(range(0, node_count, 2)) + list(range(1, node_count, 2))[::-1]

    def next_node(value):
        return lax.ppermute(value, "node", list(zip(ring, ring[1:] + ring[:1])))

    def other_x(value):
        return partner(value, "local", 1)

    mine = lax.axis_index("node") * (local_count // 2) + lax.axis_index("local") // 2
    mine = jnp.full((1,), mine, jnp.int32)
    own = (gate_weight, up_weight, down_weight)
    other = tuple(partner(weight, "local", 0) for weight in own)

    along, across = list(pack(tokens, expert_ids, gate_scores, 1)), []
    for slot in range(last):
        crossed, moved = other_x(along[slot]), next_node(along[slot])
        if slot < last - 1:
            moved = after(moved, crossed)
        if slot == last - 2:
            begun = [along[0], along[1], across[0]]
            begun = list(expert_rows(begun, mine, own, other, [rows] * 3))
            moved = after(moved, begun[0])
        along.append(moved)
        across.append(crossed)
    sizes = [rows, split, split]
    home, first_upper, first_lower = expert_rows(
        [along[2], across[1]], mine, own, other, sizes
    )
    at_home, away = [begun[0], begun[1], home], [begun[2], None]
    upper = other_x(after(along[last][:split], first_upper))
    lower = next_node(after(across[last - 1][split:], first_lower))
    middle = expert_rows([along[last], across[last - 1]], mine, own, other, [rows, rows])
    at_home.append(middle[0])

    crossed = other_x(after(first_upper, along[last][:split]))
    passed = next_node(after(first_lower, across[last - 1][split:]))
    second = [after(middle[1][:split], upper, lower), added(middle[1][split:], passed)]
    away.append(jnp.concatenate(second))
    away += expert_rows([upper, lower], mine, own, other, [rows])
    first = at_home[1]
    running = jnp.concatenate([added(first[:split], crossed), first[split:]])
    for slot in list(range(2, node_count)) + [0]:
        crossed, moved = other_x(away[slot]), next_node(running)
        running = added(at_home[slot], crossed, moved)
        if slot:
            following = (slot + 1) % node_count
            away[following] = after(away[following], crossed)
    return running


def body(tokens, expert_ids, gate_scores, gate_weight, up_weight, down_weight):
    per_group = lax.axis_size("local") // 2
    names_all = expert_ids.shape[1] == lax.axis_size("node") * per_group
    layer = dense if names_all and per_group == 2 else routed
    return layer(tokens, expert_ids, gate_scores, gate_weight, up_weight, down_weight)


def solution(mesh):
    in_specs = (
        P(("parts", "node", "local"), None),
        P(("parts", "node", "local"), None),
        P(("parts", "node", "local"), None),
        P(("node", "local"), None, None),
        P(("node", "local"), None, None),
        P(("node", "local"), None, None),
    )
    out_specs = P(("parts", "node", "local"), None)
    return jax.shard_map(body, mesh=mesh, in_specs=in_specs, out_specs=out_specs, check_vma=False)
```

```python
import functools

import jax
import jax.numpy as jnp
from jax import lax
from jax.experimental import pallas as pl
from jax.experimental.pallas import tpu as pltpu
from jax.sharding import PartitionSpec as P

TOPG = 4


def partner(value, axis, bit):
    mask = 2**bit
    pairs = [(source, source ^ mask) for source in range(lax.axis_size(axis))]
    return lax.ppermute(value, axis, pairs)


def expert_apply(arrived, gate_weight, up_weight, down_weight):
    layout = arrived.shape
    flat_rows = arrived.reshape(-1, layout[-1])
    gate_act = jnp.dot(flat_rows, gate_weight[0], preferred_element_type=jnp.float32)
    up_act = jnp.dot(flat_rows, up_weight[0], preferred_element_type=jnp.float32)
    hidden = (jax.nn.silu(gate_act) * up_act).astype(jnp.bfloat16)
    result = jnp.dot(hidden, down_weight[0], preferred_element_type=jnp.float32).astype(
        jnp.bfloat16
    )
    return result.reshape(layout)


def routed(tokens, expert_ids, gate_scores, gate_weight, up_weight, down_weight):
    rows_dev, model_width = tokens.shape
    node_count = lax.axis_size("node")
    local_count = lax.axis_size("local")
    per_group = local_count // 2
    chooser_cap = rows_dev * TOPG // node_count
    bound_most = min(chooser_cap, 3 * chooser_cap // per_group)
    group_ids = jnp.arange(node_count)
    owner_group = expert_ids // per_group
    chosen = jnp.any(owner_group[:, :, None] == group_ids[None, None, :], axis=1)
    chosen_int = chosen.astype(jnp.int32)
    before = jnp.cumsum(chosen_int, axis=0) - chosen_int
    select_one = chosen.T[:, None, :] & (
        before.T[:, None, :] == jnp.arange(chooser_cap)[None, :, None]
    )
    one_hot = select_one.astype(jnp.bfloat16)
    send_rows = jnp.einsum(
        "gsb,bd->gsd", one_hot, tokens, preferred_element_type=jnp.float32
    ).astype(jnp.bfloat16)
    token_at = jnp.sum(jnp.where(select_one, jnp.arange(rows_dev)[None, None, :], 0), axis=-1)
    occupied = jnp.any(select_one, axis=-1)
    inside = (owner_group[token_at] == group_ids[:, None, None]) & occupied[:, :, None]
    send_ids = jnp.where(inside, expert_ids[token_at] % per_group, -1)
    send_scores = jnp.where(inside, gate_scores[token_at], 0)
    arrived_rows, arrived_ids, arrived_scores = (
        lax.all_to_all(send_rows, "node", split_axis=0, concat_axis=0, tiled=True),
        lax.all_to_all(send_ids, "node", split_axis=0, concat_axis=0, tiled=True),
        lax.all_to_all(send_scores, "node", split_axis=0, concat_axis=0, tiled=True),
    )
    relayed = node_count * chooser_cap
    relay_rows = arrived_rows.reshape(relayed, model_width)
    relay_ids = arrived_ids.reshape(relayed, -1)
    relay_scores = arrived_scores.reshape(relayed, -1).astype(jnp.float32)
    member_ids = jnp.arange(per_group)
    matches = relay_ids[:, :, None] == member_ids[None, None, :]
    naming = jnp.any(matches, axis=1)
    naming_int = naming.astype(jnp.int32)
    ahead_count = jnp.cumsum(naming_int, axis=0) - naming_int
    group_cap = node_count * bound_most
    half_cap = group_cap // 2
    select_two = naming.T[:, None, :] & (
        ahead_count.T[:, None, :] == jnp.arange(group_cap)[None, :, None]
    )
    expert_rows = jnp.einsum(
        "jsr,rd->jsd",
        select_two.astype(jnp.bfloat16),
        relay_rows,
        preferred_element_type=jnp.float32,
    ).astype(jnp.bfloat16)
    outbound = expert_rows.reshape(local_count, half_cap, model_width)
    arrived = lax.all_to_all(outbound, "local", split_axis=0, concat_axis=0, tiled=True)
    partner_rows = partner(arrived, "local", 0)
    stacked = jnp.concatenate([arrived, partner_rows], axis=0)
    outputs = expert_apply(stacked, gate_weight, up_weight, down_weight)
    count = arrived.shape[0]
    mine = outputs[:count]
    theirs = outputs[count:]
    back = partner(theirs, "local", 0)
    partials = (mine.astype(jnp.float32) + back.astype(jnp.float32)).astype(jnp.bfloat16)
    returned = lax.all_to_all(partials, "local", split_axis=0, concat_axis=0, tiled=True)
    relay_weight = jnp.sum(jnp.where(matches, relay_scores[:, :, None], 0.0), axis=1)
    weighted = (jnp.transpose(select_two, (2, 0, 1)) * relay_weight[:, :, None]).astype(
        jnp.bfloat16
    )
    expert_output = returned.reshape(per_group, group_cap, model_width)
    group_sum = jnp.einsum(
        "rjs,jsd->rd", weighted, expert_output, preferred_element_type=jnp.float32
    ).astype(jnp.bfloat16)
    gathered_back = lax.all_to_all(
        group_sum.reshape(node_count, chooser_cap, model_width),
        "node",
        split_axis=0,
        concat_axis=0,
        tiled=True,
    )
    combined = jnp.einsum("gsb,gsd->bd", one_hot, gathered_back, preferred_element_type=jnp.float32)
    return combined.astype(jnp.bfloat16)

LANES = 128


def pack_kernel(tokens, expert_ids, gate_scores, *packed):
    rows, width = tokens.shape
    lane = lax.broadcasted_iota(jnp.int32, (LANES, rows), 0)
    found = jnp.zeros((LANES, rows), jnp.float32)
    for k in range(expert_ids.shape[0]):
        score = gate_scores[k : k + 1, :].astype(jnp.float32)
        found += jnp.where(lane == expert_ids[k : k + 1, :], score, 0.0)
    factors = found.T.astype(jnp.bfloat16)
    at = 0
    for out in packed:
        piece = out.shape[0]
        out[:, :width] = tokens[at : at + piece, :]
        out[:, width:] = factors[at : at + piece]
        at += piece


def pack(tokens, expert_ids, gate_scores, pieces):
    rows, width = tokens.shape
    vmem = pl.BlockSpec(memory_space=pltpu.VMEM)
    shape = jax.ShapeDtypeStruct((rows // pieces, width + LANES), tokens.dtype)
    return pl.pallas_call(
        pack_kernel,
        out_shape=[shape] * pieces,
        in_specs=[vmem] * 3,
        out_specs=[vmem] * pieces,
    )(tokens, expert_ids.T, gate_scores.T)


def expert_kernel(ranges, down_tiles, hidden_tile, mine, *refs):
    taken = len(ranges)
    blocks, weights, outs = refs[:taken], refs[taken : taken + 6], refs[taken + 6 : -6]
    rows_all, gate, up, down, hidden, sems = refs[-6:]
    width = down.shape[2]
    half = gate.shape[2]
    started = []

    def fetch(source, target):
        copy = pltpu.make_async_copy(source, target, sems.at[len(started)])
        copy.start()
        started.append(copy)
        return copy

    first, second = [], []
    for side in range(2):
        gate_hbm, up_hbm, _ = weights[3 * side : 3 * side + 3]
        for start in range(0, half, hidden_tile):
            cols = pl.ds(start, hidden_tile)
            pair = (
                fetch(gate_hbm.at[0, :, cols], gate.at[side, :, cols]),
                fetch(up_hbm.at[0, :, cols], up.at[side, :, cols]),
            )
            first.append((side, cols, pair))
    step = width // down_tiles
    for start in range(0, width, step):
        cols = pl.ds(start, step)
        pair = tuple(
            fetch(weights[3 * side + 2].at[0, :, cols], down.at[side, :, cols]) for side in range(2)
        )
        second.append((cols, pair))
    at = 0
    for block, (start, rows) in zip(blocks, ranges):
        rows_all[pl.ds(at, rows), :] = block[pl.ds(start, rows), :]
        at += rows
    lane = lax.broadcasted_iota(jnp.int32, (at, LANES), 1)
    factors = rows_all[:, width:].astype(jnp.float32)
    factor = jnp.sum(jnp.where(lane == mine[0], factors, 0.0), axis=1, keepdims=True)
    for side, cols, pair in first:
        for copy in pair:
            copy.wait()
        rows = rows_all[:, :width]
        gate_act = jnp.dot(rows, gate[side, :, cols], preferred_element_type=jnp.float32)
        up_act = jnp.dot(rows, up[side, :, cols], preferred_element_type=jnp.float32)
        hidden[side, :, cols] = (jax.nn.silu(gate_act) * up_act).astype(jnp.bfloat16)
    for cols, pair in second:
        for copy in pair:
            copy.wait()
        result = jnp.dot(hidden[0], down[0, :, cols], preferred_element_type=jnp.float32)
        result += jnp.dot(hidden[1], down[1, :, cols], preferred_element_type=jnp.float32)
        result = (result * factor).astype(jnp.bfloat16)
        at = 0
        for out in outs:
            out[:, cols] = result[at : at + out.shape[0]]
            at += out.shape[0]
    for out in outs:
        if out.shape[1] > width:
            out[:, width:] = jnp.zeros((out.shape[0], out.shape[1] - width), out.dtype)


def expert_rows(pieces, mine, own, other, outs):
    half, width = own[2].shape[1:]
    blocks = [piece[0] for piece in pieces]
    ranges = [piece[1:] for piece in pieces]
    total = sum(count for _, count in ranges)
    down_tiles = 4
    hidden_tile = half // 2
    vmem = pl.BlockSpec(memory_space=pltpu.VMEM)
    anywhere = pl.BlockSpec(memory_space=pl.ANY)
    return pl.pallas_call(
        functools.partial(expert_kernel, ranges, down_tiles, hidden_tile),
        out_shape=[jax.ShapeDtypeStruct(out, jnp.bfloat16) for out in outs],
        in_specs=[pl.BlockSpec(memory_space=pltpu.SMEM)] + [vmem] * len(blocks) + [anywhere] * 6,
        out_specs=[vmem] * len(outs),
        scratch_shapes=[
            pltpu.VMEM((total, width + LANES), jnp.bfloat16),
            pltpu.VMEM((2, width, half), jnp.bfloat16),
            pltpu.VMEM((2, width, half), jnp.bfloat16),
            pltpu.VMEM((2, half, width), jnp.bfloat16),
            pltpu.VMEM((2, total, half), jnp.bfloat16),
            pltpu.SemaphoreType.DMA((4 * (half // hidden_tile) + 2 * down_tiles,)),
        ],
        compiler_params=pltpu.CompilerParams(vmem_limit_bytes=52 * 2**20),
        cost_estimate=pl.CostEstimate(
            flops=12 * total * width * half,
            bytes_accessed=12 * width * half + 4 * total * width,
            transcendentals=2 * total * half,
        ),
    )(mine, *blocks, *own, *other)


def added(*terms):
    return sum(term.astype(jnp.float32) for term in terms).astype(jnp.bfloat16)


def after(value, *others):
    for other in others:
        same = other if other.shape == value.shape else other[:, :1]
        value = jnp.where(same == same, value, same)
    return value


def dense(tokens, expert_ids, gate_scores, gate_weight, up_weight, down_weight):
    node_count = lax.axis_size("node")
    local_count = lax.axis_size("local")
    rows, width = tokens.shape
    split = rows // 2
    last = node_count - 1

    ring = list(range(0, node_count, 2)) + list(range(1, node_count, 2))[::-1]

    def next_node(value):
        return lax.ppermute(value, "node", list(zip(ring, ring[1:] + ring[:1])))

    def other_x(value):
        return partner(value, "local", 1)

    mine = lax.axis_index("node") * (local_count // 2) + lax.axis_index("local") // 2
    mine = jnp.full((1,), mine, jnp.int32)
    own = (gate_weight, up_weight, down_weight)
    other = tuple(partner(weight, "local", 0) for weight in own)

    whole, wide = (rows, width), (split, width + LANES)

    along, across = list(pack(tokens, expert_ids, gate_scores, 1)), []
    for slot in range(last):
        crossed, moved = other_x(along[slot]), next_node(along[slot])
        if slot < last - 1:
            moved = after(moved, crossed)
        if slot == last - 2:
            pieces = [(along[0], 0, rows), (across[0], 0, rows)]
            home_own, away_own = expert_rows(pieces, mine, own, other, [whole] * 2)
            moved = after(moved, home_own)
        along.append(moved)
        across.append(crossed)
    pieces = [(along[1], 0, rows), (along[2], 0, rows), (across[1], 0, rows)]
    home_one, home_two, away_upper, away_lower = expert_rows(
        pieces, mine, own, other, [whole, whole, wide, wide]
    )

    by_x = other_x(jnp.concatenate([along[last][:split], away_upper]))
    by_node = next_node(jnp.concatenate([across[last - 1][split:], away_lower]))
    crossed, passed = by_x[split:, :width], by_node[split:, :width]
    pieces = [(along[last], 0, rows), (across[last - 1], 0, rows)]
    home_last, away_two = expert_rows(pieces, mine, own, other, [whole] * 2)

    running = jnp.concatenate([added(home_one[:split], crossed), home_one[split:]])
    away_two = jnp.concatenate(
        [after(away_two[:split], crossed), added(away_two[split:], passed)]
    )
    pieces = [(by_x, 0, split), (by_node, 0, split)]
    (away_last,) = expert_rows(pieces, mine, own, other, [whole])
    homes, aways = [home_two, home_last, home_own], [away_two, away_last, away_own]
    for i, home in enumerate(homes):
        crossed, moved = other_x(aways[i]), next_node(running)
        running = added(home, crossed, moved)
        if i < 2:
            aways[i + 1] = after(aways[i + 1], crossed)
    return running


def body(tokens, expert_ids, gate_scores, gate_weight, up_weight, down_weight):
    per_group = lax.axis_size("local") // 2
    names_all = expert_ids.shape[1] == lax.axis_size("node") * per_group
    layer = dense if names_all and per_group == 2 else routed
    return layer(tokens, expert_ids, gate_scores, gate_weight, up_weight, down_weight)


def solution(mesh):
    in_specs = (
        P(("parts", "node", "local"), None),
        P(("parts", "node", "local"), None),
        P(("parts", "node", "local"), None),
        P(("node", "local"), None, None),
        P(("node", "local"), None, None),
        P(("node", "local"), None, None),
    )
    out_specs = P(("parts", "node", "local"), None)
    return jax.shard_map(body, mesh=mesh, in_specs=in_specs, out_specs=out_specs, check_vma=False)
```

```python
import functools

import jax
import jax.numpy as jnp
from jax import lax
from jax.experimental import pallas as pl
from jax.experimental.pallas import tpu as pltpu
from jax.sharding import PartitionSpec as P

TOPG = 4


def partner(value, axis, bit):
    mask = 2**bit
    pairs = [(source, source ^ mask) for source in range(lax.axis_size(axis))]
    return lax.ppermute(value, axis, pairs)


def expert_apply(arrived, gate_weight, up_weight, down_weight):
    layout = arrived.shape
    flat_rows = arrived.reshape(-1, layout[-1])
    gate_act = jnp.dot(flat_rows, gate_weight[0], preferred_element_type=jnp.float32)
    up_act = jnp.dot(flat_rows, up_weight[0], preferred_element_type=jnp.float32)
    hidden = (jax.nn.silu(gate_act) * up_act).astype(jnp.bfloat16)
    result = jnp.dot(hidden, down_weight[0], preferred_element_type=jnp.float32).astype(
        jnp.bfloat16
    )
    return result.reshape(layout)


def routed(tokens, expert_ids, gate_scores, gate_weight, up_weight, down_weight):
    rows_dev, model_width = tokens.shape
    node_count = lax.axis_size("node")
    local_count = lax.axis_size("local")
    per_group = local_count // 2
    chooser_cap = rows_dev * TOPG // node_count
    bound_most = min(chooser_cap, 3 * chooser_cap // per_group)
    group_ids = jnp.arange(node_count)
    owner_group = expert_ids // per_group
    chosen = jnp.any(owner_group[:, :, None] == group_ids[None, None, :], axis=1)
    chosen_int = chosen.astype(jnp.int32)
    before = jnp.cumsum(chosen_int, axis=0) - chosen_int
    select_one = chosen.T[:, None, :] & (
        before.T[:, None, :] == jnp.arange(chooser_cap)[None, :, None]
    )
    one_hot = select_one.astype(jnp.bfloat16)
    send_rows = jnp.einsum(
        "gsb,bd->gsd", one_hot, tokens, preferred_element_type=jnp.float32
    ).astype(jnp.bfloat16)
    token_at = jnp.sum(jnp.where(select_one, jnp.arange(rows_dev)[None, None, :], 0), axis=-1)
    occupied = jnp.any(select_one, axis=-1)
    inside = (owner_group[token_at] == group_ids[:, None, None]) & occupied[:, :, None]
    send_ids = jnp.where(inside, expert_ids[token_at] % per_group, -1)
    send_scores = jnp.where(inside, gate_scores[token_at], 0)
    arrived_rows, arrived_ids, arrived_scores = (
        lax.all_to_all(send_rows, "node", split_axis=0, concat_axis=0, tiled=True),
        lax.all_to_all(send_ids, "node", split_axis=0, concat_axis=0, tiled=True),
        lax.all_to_all(send_scores, "node", split_axis=0, concat_axis=0, tiled=True),
    )
    relayed = node_count * chooser_cap
    relay_rows = arrived_rows.reshape(relayed, model_width)
    relay_ids = arrived_ids.reshape(relayed, -1)
    relay_scores = arrived_scores.reshape(relayed, -1).astype(jnp.float32)
    member_ids = jnp.arange(per_group)
    matches = relay_ids[:, :, None] == member_ids[None, None, :]
    naming = jnp.any(matches, axis=1)
    naming_int = naming.astype(jnp.int32)
    ahead_count = jnp.cumsum(naming_int, axis=0) - naming_int
    group_cap = node_count * bound_most
    half_cap = group_cap // 2
    select_two = naming.T[:, None, :] & (
        ahead_count.T[:, None, :] == jnp.arange(group_cap)[None, :, None]
    )
    expert_rows = jnp.einsum(
        "jsr,rd->jsd",
        select_two.astype(jnp.bfloat16),
        relay_rows,
        preferred_element_type=jnp.float32,
    ).astype(jnp.bfloat16)
    outbound = expert_rows.reshape(local_count, half_cap, model_width)
    arrived = lax.all_to_all(outbound, "local", split_axis=0, concat_axis=0, tiled=True)
    partner_rows = partner(arrived, "local", 0)
    stacked = jnp.concatenate([arrived, partner_rows], axis=0)
    outputs = expert_apply(stacked, gate_weight, up_weight, down_weight)
    count = arrived.shape[0]
    mine = outputs[:count]
    theirs = outputs[count:]
    back = partner(theirs, "local", 0)
    partials = (mine.astype(jnp.float32) + back.astype(jnp.float32)).astype(jnp.bfloat16)
    returned = lax.all_to_all(partials, "local", split_axis=0, concat_axis=0, tiled=True)
    relay_weight = jnp.sum(jnp.where(matches, relay_scores[:, :, None], 0.0), axis=1)
    weighted = (jnp.transpose(select_two, (2, 0, 1)) * relay_weight[:, :, None]).astype(
        jnp.bfloat16
    )
    expert_output = returned.reshape(per_group, group_cap, model_width)
    group_sum = jnp.einsum(
        "rjs,jsd->rd", weighted, expert_output, preferred_element_type=jnp.float32
    ).astype(jnp.bfloat16)
    gathered_back = lax.all_to_all(
        group_sum.reshape(node_count, chooser_cap, model_width),
        "node",
        split_axis=0,
        concat_axis=0,
        tiled=True,
    )
    combined = jnp.einsum("gsb,gsd->bd", one_hot, gathered_back, preferred_element_type=jnp.float32)
    return combined.astype(jnp.bfloat16)

LANES = 128


def pack_kernel(tokens, expert_ids, gate_scores, *packed):
    rows, width = tokens.shape
    lane = lax.broadcasted_iota(jnp.int32, (LANES, rows), 0)
    found = jnp.zeros((LANES, rows), jnp.float32)
    for k in range(expert_ids.shape[0]):
        score = gate_scores[k : k + 1, :].astype(jnp.float32)
        found += jnp.where(lane == expert_ids[k : k + 1, :], score, 0.0)
    factors = found.T.astype(jnp.bfloat16)
    at = 0
    for out in packed:
        piece = out.shape[0]
        out[:, :width] = tokens[at : at + piece, :]
        out[:, width:] = factors[at : at + piece]
        at += piece


def pack(tokens, expert_ids, gate_scores, pieces):
    rows, width = tokens.shape
    vmem = pl.BlockSpec(memory_space=pltpu.VMEM)
    shape = pltpu.VMEM((rows // pieces, width + LANES), tokens.dtype)
    return pl.pallas_call(
        pack_kernel,
        out_shape=[shape] * pieces,
        in_specs=[vmem] * 3,
        out_specs=[vmem] * pieces,
    )(tokens, expert_ids.T, gate_scores.T)


def expert_kernel(ranges, down_tiles, hidden_tile, mine, *refs):
    taken = len(ranges)
    blocks, weights, outs = refs[:taken], refs[taken : taken + 6], refs[taken + 6 : -6]
    rows_all, gate, up, down, hidden, sems = refs[-6:]
    width = down.shape[2]
    half = gate.shape[2]
    started = []

    def fetch(source, target):
        copy = pltpu.make_async_copy(source, target, sems.at[len(started)])
        copy.start()
        started.append(copy)
        return copy

    first, second = [], []
    for side in range(2):
        gate_hbm, up_hbm, _ = weights[3 * side : 3 * side + 3]
        for start in range(0, half, hidden_tile):
            cols = pl.ds(start, hidden_tile)
            pair = (
                fetch(gate_hbm.at[0, :, cols], gate.at[side, :, cols]),
                fetch(up_hbm.at[0, :, cols], up.at[side, :, cols]),
            )
            first.append((side, cols, pair))
    step = width // down_tiles
    for start in range(0, width, step):
        cols = pl.ds(start, step)
        pair = tuple(
            fetch(weights[3 * side + 2].at[0, :, cols], down.at[side, :, cols]) for side in range(2)
        )
        second.append((cols, pair))
    at = 0
    for block, (start, rows) in zip(blocks, ranges):
        rows_all[pl.ds(at, rows), :] = block[pl.ds(start, rows), :]
        at += rows
    lane = lax.broadcasted_iota(jnp.int32, (at, LANES), 1)
    factors = rows_all[:, width:].astype(jnp.float32)
    factor = jnp.sum(jnp.where(lane == mine[0], factors, 0.0), axis=1, keepdims=True)
    for side, cols, pair in first:
        for copy in pair:
            copy.wait()
        rows = rows_all[:, :width]
        gate_act = jnp.dot(rows, gate[side, :, cols], preferred_element_type=jnp.float32)
        up_act = jnp.dot(rows, up[side, :, cols], preferred_element_type=jnp.float32)
        hidden[side, :, cols] = (jax.nn.silu(gate_act) * up_act).astype(jnp.bfloat16)
    for cols, pair in second:
        for copy in pair:
            copy.wait()
        result = jnp.dot(hidden[0], down[0, :, cols], preferred_element_type=jnp.float32)
        result += jnp.dot(hidden[1], down[1, :, cols], preferred_element_type=jnp.float32)
        result = (result * factor).astype(jnp.bfloat16)
        at = 0
        for out in outs:
            out[:, cols] = result[at : at + out.shape[0]]
            at += out.shape[0]
    for out in outs:
        if out.shape[1] > width:
            out[:, width:] = jnp.zeros((out.shape[0], out.shape[1] - width), out.dtype)


def expert_rows(pieces, mine, own, other, outs):
    half, width = own[2].shape[1:]
    blocks = [piece[0] for piece in pieces]
    ranges = [piece[1:] for piece in pieces]
    total = sum(count for _, count in ranges)
    down_tiles = 4
    hidden_tile = half // 2
    vmem = pl.BlockSpec(memory_space=pltpu.VMEM)
    anywhere = pl.BlockSpec(memory_space=pl.ANY)
    return pl.pallas_call(
        functools.partial(expert_kernel, ranges, down_tiles, hidden_tile),
        out_shape=[jax.ShapeDtypeStruct(out, jnp.bfloat16) for out in outs],
        in_specs=[pl.BlockSpec(memory_space=pltpu.SMEM)] + [vmem] * len(blocks) + [anywhere] * 6,
        out_specs=[vmem] * len(outs),
        scratch_shapes=[
            pltpu.VMEM((total, width + LANES), jnp.bfloat16),
            pltpu.VMEM((2, width, half), jnp.bfloat16),
            pltpu.VMEM((2, width, half), jnp.bfloat16),
            pltpu.VMEM((2, half, width), jnp.bfloat16),
            pltpu.VMEM((2, total, half), jnp.bfloat16),
            pltpu.SemaphoreType.DMA((4 * (half // hidden_tile) + 2 * down_tiles,)),
        ],
        compiler_params=pltpu.CompilerParams(vmem_limit_bytes=52 * 2**20),
        cost_estimate=pl.CostEstimate(
            flops=12 * total * width * half,
            bytes_accessed=12 * width * half + 4 * total * width,
            transcendentals=2 * total * half,
        ),
    )(mine, *blocks, *own, *other)


def added(*terms):
    return sum(term.astype(jnp.float32) for term in terms).astype(jnp.bfloat16)


def after(value, *others):
    for other in others:
        same = other if other.shape == value.shape else other[:, :1]
        value = jnp.where(same == same, value, same)
    return value


def dense(tokens, expert_ids, gate_scores, gate_weight, up_weight, down_weight):
    node_count = lax.axis_size("node")
    local_count = lax.axis_size("local")
    rows, width = tokens.shape
    split = rows // 2
    last = node_count - 1

    ring = list(range(0, node_count, 2)) + list(range(1, node_count, 2))[::-1]

    def next_node(value):
        return lax.ppermute(value, "node", list(zip(ring, ring[1:] + ring[:1])))

    def other_x(value):
        return partner(value, "local", 1)

    mine = lax.axis_index("node") * (local_count // 2) + lax.axis_index("local") // 2
    mine = jnp.full((1,), mine, jnp.int32)
    own = (gate_weight, up_weight, down_weight)
    other = tuple(partner(weight, "local", 0) for weight in own)

    whole, wide = (rows, width), (split, width + LANES)

    along, across = list(pack(tokens, expert_ids, gate_scores, 1)), []
    for slot in range(last):
        crossed, moved = other_x(along[slot]), next_node(along[slot])
        if slot < last - 1:
            moved = after(moved, crossed)
        if slot == last - 2:
            pieces = [(along[0], 0, rows), (across[0], 0, rows)]
            home_own, away_own = expert_rows(pieces, mine, own, other, [whole] * 2)
            moved = after(moved, home_own)
        along.append(moved)
        across.append(crossed)
    pieces = [(along[1], 0, rows), (along[2], 0, rows), (across[1], 0, rows)]
    home_one, home_two, away_upper, away_lower = expert_rows(
        pieces, mine, own, other, [whole, whole, wide, wide]
    )

    by_x = other_x(jnp.concatenate([along[last][:split], away_upper]))
    by_node = next_node(jnp.concatenate([across[last - 1][split:], away_lower]))
    crossed, passed = by_x[split:, :width], by_node[split:, :width]
    pieces = [(along[last], 0, rows), (across[last - 1], 0, rows)]
    home_last, away_two = expert_rows(pieces, mine, own, other, [whole] * 2)

    running = jnp.concatenate([added(home_one[:split], crossed), home_one[split:]])
    away_two = jnp.concatenate(
        [after(away_two[:split], crossed), added(away_two[split:], passed)]
    )
    pieces = [(by_x, 0, split), (by_node, 0, split)]
    (away_last,) = expert_rows(pieces, mine, own, other, [whole])
    homes, aways = [home_two, home_last, home_own], [away_two, away_last, away_own]
    for i, home in enumerate(homes):
        crossed, moved = other_x(aways[i]), next_node(running)
        running = added(home, crossed, moved)
        if i < 2:
            aways[i + 1] = after(aways[i + 1], crossed)
    return running


def body(tokens, expert_ids, gate_scores, gate_weight, up_weight, down_weight):
    per_group = lax.axis_size("local") // 2
    names_all = expert_ids.shape[1] == lax.axis_size("node") * per_group
    layer = dense if names_all and per_group == 2 else routed
    return layer(tokens, expert_ids, gate_scores, gate_weight, up_weight, down_weight)


def solution(mesh):
    in_specs = (
        P(("parts", "node", "local"), None),
        P(("parts", "node", "local"), None),
        P(("parts", "node", "local"), None),
        P(("node", "local"), None, None),
        P(("node", "local"), None, None),
        P(("node", "local"), None, None),
    )
    out_specs = P(("parts", "node", "local"), None)
    return jax.shard_map(body, mesh=mesh, in_specs=in_specs, out_specs=out_specs, check_vma=False)
```
